512 devices in a mesh: day: 4 (over z_hi), row: 16 (over y, z_lo), col: 8 (over x, core).
Axes of the slice: x: 4, y: 4, z: 16 (z_hi: 4, z_lo: 4; z = z_hi * 4 + z_lo), core: 2. Of those that a mesh axis runs over, the one named last changes fastest.
Arguments:
- returns: float32 [8, 512, 8192], P('day', None, ('row', 'col')), may hold values from -100 to 100
- traded: int32 [8, 512, 8192], P('day', None, ('row', 'col')), may hold values 0 or 1
Outputs:
- covariance: float32 [8, 8192, 8192], P('day', 'row', 'col')
The draws below stay inside these ranges and needn't reach their ends.
All inputs are finite; a program needn't handle non-finite values. No bound on the sum of `traded` on one device may be relied on, other than what follows from the above.
Results may differ from the reference program's by a relative error of at most 0.000086.
Values sent between devices are 32-bit elements; how exact they have to be, the bound alone decides.
No kernel may reach another device: no remote copies, remote signals or barrier semaphores. Data moves between devices by JAX's collectives and lax.ppermute only.
A program may use at most 64 MiB of HBM per device.

```python
import jax
import jax.numpy as jnp
from jax import lax

ASSETS = 8192
BINS = 512
DAYS = 8


def draw_returns(key, part):
    key = jax.random.fold_in(key, 11)
    keys = jax.random.split(key, 4)
    vol = jnp.exp(jax.random.uniform(keys[0], (1, 1, ASSETS), jnp.float32, jnp.log(0.5), jnp.log(2.0)))
    day_scale = jnp.exp(jax.random.uniform(keys[1], (DAYS, 1, ASSETS), jnp.float32, jnp.log(0.6), jnp.log(1.6)))
    position = jnp.arange(BINS, dtype=jnp.float32) / BINS
    shape_curve = (1.0 + 2.0 * (2.0 * position - 1.0) ** 2).reshape(1, BINS, 1)
    market = jnp.clip(jax.random.normal(keys[2], (DAYS, BINS, 1), jnp.float32), -5.0, 5.0)
    noise = jnp.clip(jax.random.normal(keys[3], (DAYS, BINS, ASSETS), jnp.float32), -5.0, 5.0)
    common = 0.5
    values = vol * day_scale * shape_curve * (common * market + noise) / jnp.sqrt(jnp.float32(BINS))
    return values.astype(jnp.float32)


def set_ends(result, stream_key, low, high):
    longest = result.shape.index(max(result.shape))
    spots = []
    for shift in (0, 1):
        where = [jax.random.randint(jax.random.fold_in(stream_key, axis), (), 0, length) for axis, length in enumerate(result.shape)]
        where[longest] = (where[longest] + shift) % result.shape[longest]
        spots.append(tuple(where))
    return result.at[spots[0]].set(low).at[spots[1]].set(high)


def setup_inputs(seed: int = 0) -> dict:
    key_of = jax.random.split(jax.random.key(seed), 3)
    return {
        "returns": draw_returns(jax.random.fold_in(key_of[2], 71), 0),
        "traded": set_ends((jax.random.randint(key_of[1], (DAYS, BINS, ASSETS), 0, 4) < 3).astype(jnp.int32), jax.random.fold_in(key_of[1], 1), 0, 1),
    }


def reference(returns, traded):
    live = traded.astype(jnp.float32)
    absolute = lax.optimization_barrier(jnp.sum(live * jnp.abs(returns), axis=0))
    count = lax.optimization_barrier(jnp.sum(live, axis=0))
    level = absolute / jnp.maximum(count, 1.0)
    profile = level / jnp.sqrt(lax.optimization_barrier(jnp.mean(level * level, axis=0, keepdims=True)) + 1e-06)
    scaled = live * returns / jnp.maximum(profile, 0.2)

    def one_day(panel):
        return jnp.dot(panel.T, panel, preferred_element_type=jnp.float32, precision=lax.Precision.HIGHEST)
    return lax.map(one_day, scaled)
```

```python
import jax
import jax.numpy as jnp
from jax import lax
from jax.experimental import pallas as pl
from jax.experimental.pallas import tpu as pltpu
from jax.sharding import Mesh
from jax.sharding import PartitionSpec as P

DAY, Y, Z, X, CORE = "day", "y", "z", "x", "core"
SIZES = (4, 4, 4, 4, 2)
ALL = (DAY, Y, Z, X, CORE)
GROUP = (Y, Z, X, CORE)
N = 4
WHOLE = pl.BlockSpec(memory_space=pltpu.VMEM)
SCALARS = pl.BlockSpec(memory_space=pltpu.SMEM)


def turn_pairs():
    def place(y, z, x, core):
        return ((y * N + z) * N + x) * 2 + core

    pairs = []
    for y in range(N):
        for z in range(N):
            for x in range(N):
                for core in range(2):
                    pairs.append((place(y, z, x, core), place(x, (z % 2) * 2 + core, y, z // 2)))
    return pairs


def shift(step):
    return [(i, (i + step) % N) for i in range(N)]


def local(kernel, shapes, *blocks, after=(), specs=None):
    skip = len(after)

    def run(*refs):
        kernel(*refs[: len(blocks)], *refs[len(blocks) + skip :])

    moved = sum(4 * block.size for block in blocks) + sum(4 * shape.size for shape in shapes)
    return pl.pallas_call(
        run,
        in_specs=(specs or [WHOLE] * len(blocks)) + [pl.BlockSpec(memory_space=pl.ANY)] * skip,
        out_specs=[WHOLE] * len(shapes),
        out_shape=shapes,
        compiler_params=pltpu.CompilerParams(vmem_limit_bytes=8 * 1024 * 1024),
        cost_estimate=pl.CostEstimate(flops=moved, bytes_accessed=moved, transcendentals=0),
    )(*blocks, *after)


def sums_kernel(returns, traded, masked, sums):
    share = sums.shape[2]
    for group in range(N):
        rows = slice(group * share, (group + 1) * share)
        absolute = jnp.zeros(sums.shape[2:], jnp.float32)
        count = jnp.zeros(sums.shape[2:], jnp.float32)
        for k in range(masked.shape[0]):
            live = traded[k, rows, :].astype(jnp.float32)
            value = live * returns[k, rows, :]
            masked[k, rows, :] = value
            absolute += jnp.abs(value)
            count += live
        sums[group, 0] = absolute
        sums[group, 1] = count


def weight_kernel(sums, weight):
    absolute = (sums[0, 0] + sums[1, 0]) + (sums[2, 0] + sums[3, 0])
    count = (sums[0, 1] + sums[1, 1]) + (sums[2, 1] + sums[3, 1])
    level = absolute / jnp.maximum(count, 1.0)
    profile = level / jnp.sqrt(jnp.mean(level * level, axis=1, keepdims=True) + 1e-06)
    weight[...] = 1.0 / jnp.maximum(profile, 0.2)


def scale_kernel(masked, weight, scaled):
    for k in range(masked.shape[0]):
        scaled[k] = masked[k] * weight[...]


def pack_kernel(z1, z2, z3, y_up, y_down, up, down):
    for n, piece in enumerate((z1, z2, z3)):
        for k in range(2):
            up[2 * n + k] = piece[k]
            down[2 * n + k] = piece[k]
    up[6] = y_up[0]
    down[6] = y_down[1]


def hand_on_kernel(from_up, from_down, up, down):
    for n, (here, there) in enumerate(((0, 4), (1, 5), (2, 3))):
        up[n] = from_up[here]
        down[n] = from_down[there]


def split(value):
    high = value.astype(jnp.bfloat16)
    low = (value - high.astype(jnp.float32)).astype(jnp.bfloat16)
    return high, low


def triple(row_high, row_low, col_high, col_low):
    def dot(left, right):
        return lax.dot_general(left, right, (((1,), (1,)), ((), ())), preferred_element_type=jnp.float32)

    return dot(row_high, col_low) + dot(row_low, col_high) + dot(row_high, col_high)


def keep_columns(where, step, blocks, high, low):
    size = blocks[0].shape[0]
    for n, block in enumerate(blocks):
        part = pl.ds(pl.multiple_of(lax.rem(where[1] - n + N, N) * size, size), size)
        high[step, part, :], low[step, part, :] = split(block)


def send_columns(where, step, k, tile, out, sems):
    half = tile.shape[1] // 2
    x = lax.rem(where[0] - step + N, N)
    copies = []
    for p in range(2):
        start = pl.multiple_of((p * N + x) * half, half)
        copies.append(
            pltpu.make_async_copy(tile.at[:, p * half : (p + 1) * half], out.at[k, :, pl.ds(start, half)], sems.at[p])
        )
    return copies


def near_kernel(
    where, rows, own, z1, z2, z3, y_up, up, y_down, down, out, row_high, row_low, high, low, tiles, sems
):
    size = rows.shape[2]
    copies = []
    for k in range(2):
        for n in range(rows.shape[0]):
            part = slice(n * size, (n + 1) * size)
            row_high[k, part, :], row_low[k, part, :] = split(rows[n, k])
        groups = (
            (0, [own[k], z1[k], z2[k], z3[k]]),
            (1, [y_up[k], up[k], up[2 + k], up[4 + k]]),
            (3, [y_down[k], down[k], down[2 + k], down[4 + k]]),
        )
        for n, (step, blocks) in enumerate(groups):
            spot = 3 * k + n
            keep_columns(where, spot, blocks, high, low)
            tiles[k, n] = triple(row_high[k], row_low[k], high[spot], low[spot])
            for copy in send_columns(where, step, k, tiles.at[k, n], out, sems.at[k, n]):
                copy.start()
                copies.append(copy)
    for copy in copies:
        copy.wait()


def far_kernel(where, row_high, row_low, up, down, far_up, far_down, kept, out, high, low, tiles, sems):
    blocks = (
        [up[6], far_up[0], far_up[2], far_down[0]],
        [down[6], far_up[1], far_down[2], far_down[1]],
    )
    copies = []
    for k in range(2):
        keep_columns(where, k, blocks[k], high, low)
        tiles[k] = triple(row_high[k], row_low[k], high[k], low[k])
        for copy in send_columns(where, 2, k, tiles.at[k], out, sems.at[k]):
            copy.start()
            copies.append(copy)
    for copy in copies:
        copy.wait()


def near_product(where, rows, *blocks):
    _, days, size, bins = rows.shape
    height, width = rows.shape[0] * size, N * size
    halves = [jax.ShapeDtypeStruct((days, height, bins), jnp.bfloat16)] * 2
    return pl.pallas_call(
        near_kernel,
        in_specs=[SCALARS] + [WHOLE] * (1 + len(blocks)),
        out_specs=[pl.BlockSpec(memory_space=pl.ANY), WHOLE, WHOLE],
        out_shape=[jax.ShapeDtypeStruct((days, height, N * width), jnp.float32)] + halves,
        scratch_shapes=[
            pltpu.VMEM((3 * days, width, bins), jnp.bfloat16),
            pltpu.VMEM((3 * days, width, bins), jnp.bfloat16),
            pltpu.VMEM((days, 3, height, width), jnp.float32),
            pltpu.SemaphoreType.DMA((days, 3, 2)),
        ],
        compiler_params=pltpu.CompilerParams(vmem_limit_bytes=16 * 1024 * 1024),
        cost_estimate=pl.CostEstimate(
            flops=18 * days * height * width * bins, bytes_accessed=12 * days * height * width, transcendentals=0
        ),
    )(where, rows, *blocks)


def far_product(where, row_high, row_low, up, down, far_up, far_down, kept):
    days, height, bins = row_high.shape
    width = kept.shape[2] // N
    anywhere = pl.BlockSpec(memory_space=pl.ANY)
    return pl.pallas_call(
        far_kernel,
        in_specs=[SCALARS] + [WHOLE] * 6 + [anywhere],
        out_specs=anywhere,
        out_shape=jax.ShapeDtypeStruct(kept.shape, kept.dtype),
        input_output_aliases={7: 0},
        scratch_shapes=[
            pltpu.VMEM((days, width, bins), jnp.bfloat16),
            pltpu.VMEM((days, width, bins), jnp.bfloat16),
            pltpu.VMEM((days, height, width), jnp.float32),
            pltpu.SemaphoreType.DMA((days, 2)),
        ],
        compiler_params=pltpu.CompilerParams(vmem_limit_bytes=8 * 1024 * 1024),
        cost_estimate=pl.CostEstimate(
            flops=6 * days * height * width * bins, bytes_accessed=4 * days * height * width, transcendentals=0
        ),
    )(where, row_high, row_low, up, down, far_up, far_down, kept)


def body(returns, traded):
    returns = jnp.swapaxes(returns, 1, 2)
    traded = jnp.swapaxes(traded, 1, 2)
    days, size, bins = returns.shape
    share = size // N

    def shape(*sizes):
        return jax.ShapeDtypeStruct(sizes, jnp.float32)

    masked, sums = local(
        sums_kernel, [shape(days, size, bins), shape(N, 2, share, bins)], returns, traded, specs=[pl.BlockSpec()] * 2
    )
    sums = lax.all_to_all(sums, DAY, 0, 0)
    (weight,) = local(weight_kernel, [shape(share, bins)], sums)
    weight = lax.all_gather(weight, DAY, axis=0, tiled=True)
    (scaled,) = local(scale_kernel, [shape(days, size, bins)], masked, weight)

    rows = lax.all_gather(scaled, (X, CORE))

    turned = lax.ppermute(scaled, GROUP, turn_pairs())
    z_pieces = [lax.ppermute(turned, Z, shift(step)) for step in (1, 2, 3)]
    y_up = lax.ppermute(turned, Y, shift(1))
    y_down = lax.ppermute(turned, Y, shift(-1))
    up, down = local(pack_kernel, [shape(7, size, bins)] * 2, *z_pieces, y_up, y_down)
    up = lax.ppermute(up, Y, shift(1))
    down = lax.ppermute(down, Y, shift(-1))
    far_up, far_down = local(hand_on_kernel, [shape(3, size, bins)] * 2, up, down)
    far_up = lax.ppermute(far_up, Y, shift(1))
    far_down = lax.ppermute(far_down, Y, shift(-1))

    where = jnp.stack([lax.axis_index(Y), lax.axis_index(Z)]).astype(jnp.int32)
    out, row_high, row_low = near_product(where, rows, turned, *z_pieces, y_up, up, y_down, down)
    return far_product(where, row_high, row_low, up, down, far_up, far_down, out)


def solution(mesh):
    fine = Mesh(mesh.devices.reshape(SIZES), ALL)
    in_spec = P(DAY, None, GROUP)
    return jax.shard_map(
        body,
        mesh=fine,
        in_specs=(in_spec, in_spec),
        out_specs=P(DAY, (Y, Z), (X, CORE)),
        check_vma=False,
    )
```

```python
import jax
import jax.numpy as jnp
from jax import lax
from jax.experimental import pallas as pl
from jax.experimental.pallas import tpu as pltpu
from jax.sharding import Mesh
from jax.sharding import PartitionSpec as P

DAY, Y, Z, X, CORE = "day", "y", "z", "x", "core"
SIZES = (4, 4, 4, 4, 2)
ALL = (DAY, Y, Z, X, CORE)
GROUP = (Y, Z, X, CORE)
N = 4
WHOLE = pl.BlockSpec(memory_space=pltpu.VMEM)
SCALARS = pl.BlockSpec(memory_space=pltpu.SMEM)


def turn_pairs():
    def place(y, z, x, core):
        return ((y * N + z) * N + x) * 2 + core

    pairs = []
    for y in range(N):
        for z in range(N):
            for x in range(N):
                for core in range(2):
                    pairs.append((place(y, z, x, core), place(x, (z % 2) * 2 + core, y, z // 2)))
    return pairs


def shift(step):
    return [(i, (i + step) % N) for i in range(N)]


def ring_pairs():
    return [(y * 2 + core, (y + (1, N - 1)[core]) % N * 2 + core) for y in range(N) for core in range(2)]


def local(kernel, shapes, *blocks, after=(), specs=None, scratch=()):
    skip = len(after)

    def run(*refs):
        kernel(*refs[: len(blocks)], *refs[len(blocks) + skip :])

    moved = sum(4 * block.size for block in blocks) + sum(4 * shape.size for shape in shapes)
    return pl.pallas_call(
        run,
        in_specs=(specs or [WHOLE] * len(blocks)) + [pl.BlockSpec(memory_space=pl.ANY)] * skip,
        out_specs=[WHOLE] * len(shapes),
        out_shape=shapes,
        scratch_shapes=scratch,
        compiler_params=pltpu.CompilerParams(vmem_limit_bytes=8 * 1024 * 1024),
        cost_estimate=pl.CostEstimate(flops=moved, bytes_accessed=moved, transcendentals=0),
    )(*blocks, *after)


def sums_kernel(returns_far, traded_far, masked, sums, returns, traded, sems):
    copies = [
        pltpu.make_async_copy(returns_far, returns, sems.at[0]),
        pltpu.make_async_copy(traded_far, traded, sems.at[1]),
    ]
    for copy in copies:
        copy.start()
    for copy in copies:
        copy.wait()
    share = sums.shape[2]
    for group in range(N):
        rows = slice(group * share, (group + 1) * share)
        absolute = jnp.zeros(sums.shape[2:], jnp.float32)
        count = jnp.zeros(sums.shape[2:], jnp.float32)
        for k in range(masked.shape[0]):
            live = traded[k, rows, :].astype(jnp.float32)
            value = live * returns[k, rows, :]
            masked[k, rows, :] = value
            absolute += jnp.abs(value)
            count += live
        sums[group, 0] = absolute
        sums[group, 1] = count


def weight_kernel(sums, weight):
    absolute = (sums[0, 0] + sums[1, 0]) + (sums[2, 0] + sums[3, 0])
    count = (sums[0, 1] + sums[1, 1]) + (sums[2, 1] + sums[3, 1])
    level = absolute / jnp.maximum(count, 1.0)
    profile = level / jnp.sqrt(jnp.mean(level * level, axis=1, keepdims=True) + 1e-06)
    weight[...] = 1.0 / jnp.maximum(profile, 0.2)


def scale_kernel(masked, weight, scaled):
    for k in range(masked.shape[0]):
        scaled[k] = masked[k] * weight[...]


def pair_kernel(first, second, out):
    out[:2] = first[...]
    out[2:] = second[...]


def split(value):
    high = value.astype(jnp.bfloat16)
    low = (value - high.astype(jnp.float32)).astype(jnp.bfloat16)
    return high, low


def triple(row_high, row_low, col_high, col_low):
    def dot(left, right):
        return lax.dot_general(left, right, (((1,), (1,)), ((), ())), preferred_element_type=jnp.float32)

    return dot(row_high, col_low) + dot(row_low, col_high) + dot(row_high, col_high)


def keep_columns(where, step, blocks, high, low):
    size = blocks[0].shape[0]
    for n, block in enumerate(blocks):
        part = pl.ds(pl.multiple_of(lax.rem(where[1] - n + N, N) * size, size), size)
        high[step, part, :], low[step, part, :] = split(block)


def send_columns(where, step, k, tile, out, sems):
    half = tile.shape[1] // 2
    x = lax.rem(where[0] + step * where[2], N)
    copies = []
    for p in range(2):
        start = pl.multiple_of((p * N + x) * half, half)
        copies.append(
            pltpu.make_async_copy(tile.at[:, p * half : (p + 1) * half], out.at[k, :, pl.ds(start, half)], sems.at[p])
        )
    return copies


def near_kernel(
    where, rows, a, b, a_one, b_one, a_two, b_two, out, row_high, row_low, high, low, tiles, sems
):
    size = rows.shape[2]
    copies = []
    for k in range(2):
        for n in range(rows.shape[0]):
            part = slice(n * size, (n + 1) * size)
            row_high[k, part, :], row_low[k, part, :] = split(rows[n, k])
        for step, (here, there) in enumerate(((a, b), (a_one, b_one), (a_two, b_two))):
            blocks = [there[k], there[2 + k], here[k], here[2 + k]]
            spot = 3 * k + step
            keep_columns(where, spot, blocks, high, low)
            tiles[k, step] = triple(row_high[k], row_low[k], high[spot], low[spot])
            for copy in send_columns(where, step, k, tiles.at[k, step], out, sems.at[k, step]):
                copy.start()
                copies.append(copy)
    for copy in copies:
        copy.wait()


def far_kernel(where, row_high, row_low, a, b, kept, out, high, low, tiles, sems):
    copies = []
    for k in range(2):
        keep_columns(where, k, [b[k], b[2 + k], a[k], a[2 + k]], high, low)
        tiles[k] = triple(row_high[k], row_low[k], high[k], low[k])
        for copy in send_columns(where, 3, k, tiles.at[k], out, sems.at[k]):
            copy.start()
            copies.append(copy)
    for copy in copies:
        copy.wait()


def near_product(where, rows, *blocks):
    _, days, size, bins = rows.shape
    height, width = rows.shape[0] * size, N * size
    halves = [jax.ShapeDtypeStruct((days, height, bins), jnp.bfloat16)] * 2
    return pl.pallas_call(
        near_kernel,
        in_specs=[SCALARS] + [WHOLE] * (1 + len(blocks)),
        out_specs=[pl.BlockSpec(memory_space=pl.ANY), WHOLE, WHOLE],
        out_shape=[jax.ShapeDtypeStruct((days, height, N * width), jnp.float32)] + halves,
        scratch_shapes=[
            pltpu.VMEM((3 * days, width, bins), jnp.bfloat16),
            pltpu.VMEM((3 * days, width, bins), jnp.bfloat16),
            pltpu.VMEM((days, 3, height, width), jnp.float32),
            pltpu.SemaphoreType.DMA((days, 3, 2)),
        ],
        compiler_params=pltpu.CompilerParams(vmem_limit_bytes=16 * 1024 * 1024),
        cost_estimate=pl.CostEstimate(
            flops=18 * days * height * width * bins, bytes_accessed=12 * days * height * width, transcendentals=0
        ),
    )(where, rows, *blocks)


def far_product(where, row_high, row_low, a, b, kept):
    days, height, bins = row_high.shape
    width = kept.shape[2] // N
    anywhere = pl.BlockSpec(memory_space=pl.ANY)
    return pl.pallas_call(
        far_kernel,
        in_specs=[SCALARS] + [WHOLE] * 4 + [anywhere],
        out_specs=anywhere,
        out_shape=jax.ShapeDtypeStruct(kept.shape, kept.dtype),
        input_output_aliases={5: 0},
        scratch_shapes=[
            pltpu.VMEM((days, width, bins), jnp.bfloat16),
            pltpu.VMEM((days, width, bins), jnp.bfloat16),
            pltpu.VMEM((days, height, width), jnp.float32),
            pltpu.SemaphoreType.DMA((days, 2)),
        ],
        compiler_params=pltpu.CompilerParams(vmem_limit_bytes=8 * 1024 * 1024),
        cost_estimate=pl.CostEstimate(
            flops=6 * days * height * width * bins, bytes_accessed=4 * days * height * width, transcendentals=0
        ),
    )(where, row_high, row_low, a, b, kept)


def body(returns, traded):
    returns = jnp.swapaxes(returns, 1, 2)
    traded = jnp.swapaxes(traded, 1, 2)
    days, size, bins = returns.shape
    share = size // N

    def shape(*sizes):
        return jax.ShapeDtypeStruct(sizes, jnp.float32)

    masked, sums = local(
        sums_kernel,
        [shape(days, size, bins), shape(N, 2, share, bins)],
        returns,
        traded,
        specs=[pl.BlockSpec(memory_space=pltpu.HBM)] * 2,
        scratch=[
            pltpu.VMEM((days, size, bins), jnp.float32),
            pltpu.VMEM((days, size, bins), jnp.int32),
            pltpu.SemaphoreType.DMA((2,)),
        ],
    )
    sums = lax.all_to_all(sums, DAY, 0, 0)
    (weight,) = local(weight_kernel, [shape(share, bins)], sums)
    weight = lax.all_gather(weight, DAY, axis=0, tiled=True)
    (scaled,) = local(scale_kernel, [shape(days, size, bins)], masked, weight)

    rows = lax.all_gather(scaled, (X, CORE))

    turned = lax.ppermute(scaled, GROUP, turn_pairs())
    z1, z2, z3 = [lax.ppermute(turned, Z, shift(step)) for step in (1, 2, 3)]
    (b,) = local(pair_kernel, [shape(4, size, bins)], turned, z1)
    (a,) = local(pair_kernel, [shape(4, size, bins)], z2, z3)
    units = [a, b]
    for _ in range(N - 1):
        units += [lax.ppermute(unit, (Y, CORE), ring_pairs()) for unit in units[-2:]]

    back = lax.select(lax.axis_index(CORE) == 0, N - 1, 1)
    where = jnp.stack([lax.axis_index(Y), lax.axis_index(Z), back]).astype(jnp.int32)
    out, row_high, row_low = near_product(where, rows, *units[:6])
    return far_product(where, row_high, row_low, *units[6:], out)


def solution(mesh):
    fine = Mesh(mesh.devices.reshape(SIZES), ALL)
    in_spec = P(DAY, None, GROUP)
    return jax.shard_map(
        body,
        mesh=fine,
        in_specs=(in_spec, in_spec),
        out_specs=P(DAY, (Y, Z), (X, CORE)),
        check_vma=False,
    )
```

```python
import jax
import jax.numpy as jnp
from jax import lax
from jax.experimental import pallas as pl
from jax.experimental.pallas import tpu as pltpu
from jax.sharding import Mesh
from jax.sharding import PartitionSpec as P

DAY, Y, Z, X, CORE = "day", "y", "z", "x", "core"
SIZES = (4, 4, 4, 4, 2)
ALL = (DAY, Y, Z, X, CORE)
GROUP = (Y, Z, X, CORE)
N = 4
WHOLE = pl.BlockSpec(memory_space=pltpu.VMEM)
SCALARS = pl.BlockSpec(memory_space=pltpu.SMEM)


def turn_pairs():
    def place(y, z, x, core):
        return ((y * N + z) * N + x) * 2 + core

    pairs = []
    for y in range(N):
        for z in range(N):
            for x in range(N):
                for core in range(2):
                    pairs.append((place(y, z, x, core), place(x, (z % 2) * 2 + core, y, z // 2)))
    return pairs


def shift(step):
    return [(i, (i + step) % N) for i in range(N)]


def ring_pairs():
    return [(y * 2 + core, (y + (1, N - 1)[core]) % N * 2 + core) for y in range(N) for core in range(2)]


def local(kernel, shapes, *blocks, after=(), specs=None, scratch=(), limit=8):
    skip = len(after)

    def run(*refs):
        kernel(*refs[: len(blocks)], *refs[len(blocks) + skip :])

    moved = sum(4 * block.size for block in blocks) + sum(4 * shape.size for shape in shapes)
    return pl.pallas_call(
        run,
        in_specs=(specs or [WHOLE] * len(blocks)) + [pl.BlockSpec(memory_space=pl.ANY)] * skip,
        out_specs=[WHOLE] * len(shapes),
        out_shape=shapes,
        scratch_shapes=scratch,
        compiler_params=pltpu.CompilerParams(vmem_limit_bytes=limit * 1024 * 1024),
        cost_estimate=pl.CostEstimate(flops=moved, bytes_accessed=moved, transcendentals=0),
    )(*blocks, *after)


def sums_kernel(returns_far, traded_far, masked, sums, returns, traded, sems):
    copies = [
        pltpu.make_async_copy(returns_far, returns, sems.at[0]),
        pltpu.make_async_copy(traded_far, traded, sems.at[1]),
    ]
    for copy in copies:
        copy.start()
    for copy in copies:
        copy.wait()
    share = sums.shape[2]
    for group in range(N):
        rows = slice(group * share, (group + 1) * share)
        absolute = jnp.zeros(sums.shape[2:], jnp.float32)
        count = jnp.zeros(sums.shape[2:], jnp.float32)
        for k in range(masked.shape[0]):
            live = traded[k, rows, :].astype(jnp.float32)
            value = live * returns[k, rows, :]
            masked[k, rows, :] = value
            absolute += jnp.abs(value)
            count += live
        sums[group, 0] = absolute
        sums[group, 1] = count


def weight_kernel(sums, weight):
    absolute = (sums[0, 0] + sums[1, 0]) + (sums[2, 0] + sums[3, 0])
    count = (sums[0, 1] + sums[1, 1]) + (sums[2, 1] + sums[3, 1])
    level = absolute / jnp.maximum(count, 1.0)
    profile = level / jnp.sqrt(jnp.mean(level * level, axis=1, keepdims=True) + 1e-06)
    weight[...] = 1.0 / jnp.maximum(profile, 0.2)


def scale_kernel(masked, weight, scaled):
    for k in range(masked.shape[0]):
        scaled[k] = masked[k] * weight[...]


def pair_kernel(first, second, out):
    out[:2] = first[...]
    out[2:] = second[...]


def split(value):
    high = value.astype(jnp.bfloat16)
    low = (value - high.astype(jnp.float32)).astype(jnp.bfloat16)
    return high, low


def triple(row_high, row_low, col_high, col_low):
    def dot(left, right):
        return lax.dot_general(left, right, (((1,), (1,)), ((), ())), preferred_element_type=jnp.float32)

    return dot(row_high, col_low) + dot(row_low, col_high) + dot(row_high, col_high)


def keep_columns(where, step, blocks, high, low):
    size = blocks[0].shape[0]
    for n, block in enumerate(blocks):
        part = pl.ds(pl.multiple_of(lax.rem(where[1] - n + N, N) * size, size), size)
        high[step, part, :], low[step, part, :] = split(block)


def send_columns(where, step, k, tile, out, sems):
    half = tile.shape[1] // 2
    x = lax.rem(where[0] + step * where[2], N)
    copies = []
    for p in range(2):
        start = pl.multiple_of((p * N + x) * half, half)
        copies.append(
            pltpu.make_async_copy(tile.at[:, p * half : (p + 1) * half], out.at[k, :, pl.ds(start, half)], sems.at[p])
        )
    return copies


def near_kernel(
    where, rows, a, b, a_one, b_one, a_two, b_two, out, row_high, row_low, high, low, tiles, sems
):
    size = rows.shape[2]
    copies = []
    for k in range(2):
        for n in range(rows.shape[0]):
            part = slice(n * size, (n + 1) * size)
            row_high[k, part, :], row_low[k, part, :] = split(rows[n, k])
        for step, (here, there) in enumerate(((a, b), (a_one, b_one), (a_two, b_two))):
            blocks = [there[k], there[2 + k], here[k], here[2 + k]]
            spot = 3 * k + step
            keep_columns(where, spot, blocks, high, low)
            tiles[k, step] = triple(row_high[k], row_low[k], high[spot], low[spot])
            for copy in send_columns(where, step, k, tiles.at[k, step], out, sems.at[k, step]):
                copy.start()
                copies.append(copy)
    for copy in copies:
        copy.wait()


def far_kernel(where, row_high, row_low, a, b, kept, out, high, low, tiles, sems):
    copies = []
    for k in range(2):
        keep_columns(where, k, [b[k], b[2 + k], a[k], a[2 + k]], high, low)
        tiles[k] = triple(row_high[k], row_low[k], high[k], low[k])
        for copy in send_columns(where, 3, k, tiles.at[k], out, sems.at[k]):
            copy.start()
            copies.append(copy)
    for copy in copies:
        copy.wait()


def near_product(where, rows, *blocks):
    _, days, size, bins = rows.shape
    height, width = rows.shape[0] * size, N * size
    halves = [jax.ShapeDtypeStruct((days, height, bins), jnp.bfloat16)] * 2
    return pl.pallas_call(
        near_kernel,
        in_specs=[SCALARS] + [WHOLE] * (1 + len(blocks)),
        out_specs=[pl.BlockSpec(memory_space=pl.ANY), WHOLE, WHOLE],
        out_shape=[jax.ShapeDtypeStruct((days, height, N * width), jnp.float32)] + halves,
        scratch_shapes=[
            pltpu.VMEM((3 * days, width, bins), jnp.bfloat16),
            pltpu.VMEM((3 * days, width, bins), jnp.bfloat16),
            pltpu.VMEM((days, 3, height, width), jnp.float32),
            pltpu.SemaphoreType.DMA((days, 3, 2)),
        ],
        compiler_params=pltpu.CompilerParams(vmem_limit_bytes=16 * 1024 * 1024),
        cost_estimate=pl.CostEstimate(
            flops=18 * days * height * width * bins, bytes_accessed=12 * days * height * width, transcendentals=0
        ),
    )(where, rows, *blocks)


def far_product(where, row_high, row_low, a, b, kept):
    days, height, bins = row_high.shape
    width = kept.shape[2] // N
    anywhere = pl.BlockSpec(memory_space=pl.ANY)
    return pl.pallas_call(
        far_kernel,
        in_specs=[SCALARS] + [WHOLE] * 4 + [anywhere],
        out_specs=anywhere,
        out_shape=jax.ShapeDtypeStruct(kept.shape, kept.dtype),
        input_output_aliases={5: 0},
        scratch_shapes=[
            pltpu.VMEM((days, width, bins), jnp.bfloat16),
            pltpu.VMEM((days, width, bins), jnp.bfloat16),
            pltpu.VMEM((days, height, width), jnp.float32),
            pltpu.SemaphoreType.DMA((days, 2)),
        ],
        compiler_params=pltpu.CompilerParams(vmem_limit_bytes=8 * 1024 * 1024),
        cost_estimate=pl.CostEstimate(
            flops=6 * days * height * width * bins, bytes_accessed=4 * days * height * width, transcendentals=0
        ),
    )(where, row_high, row_low, a, b, kept)


def body(returns, traded):
    returns = jnp.swapaxes(returns, 1, 2)
    traded = jnp.swapaxes(traded, 1, 2)
    days, size, bins = returns.shape
    share = size // N

    def shape(*sizes):
        return jax.ShapeDtypeStruct(sizes, jnp.float32)

    masked, sums = local(
        sums_kernel,
        [shape(days, size, bins), shape(N, 2, share, bins)],
        returns,
        traded,
        specs=[pl.BlockSpec(memory_space=pltpu.HBM)] * 2,
        scratch=[
            pltpu.VMEM((days, size, bins), jnp.float32),
            pltpu.VMEM((days, size, bins), jnp.int32),
            pltpu.SemaphoreType.DMA((2,)),
        ],
        limit=60,
    )
    sums = lax.all_to_all(sums, DAY, 0, 0)
    (weight,) = local(weight_kernel, [shape(share, bins)], sums)
    weight = lax.all_gather(weight, DAY, axis=0, tiled=True)
    (scaled,) = local(scale_kernel, [shape(days, size, bins)], masked, weight)

    turned = lax.ppermute(scaled, GROUP, turn_pairs())

    rows = lax.all_gather(lax.optimization_barrier((scaled, turned))[0], (X, CORE))

    z1, z2, z3 = [lax.ppermute(turned, Z, shift(step)) for step in (1, 2, 3)]
    (b,) = local(pair_kernel, [shape(4, size, bins)], turned, z1)
    (a,) = local(pair_kernel, [shape(4, size, bins)], z2, z3)
    units = [a, b]
    for _ in range(N - 1):
        units += [lax.ppermute(unit, (Y, CORE), ring_pairs()) for unit in units[-2:]]

    back = lax.select(lax.axis_index(CORE) == 0, N - 1, 1)
    where = jnp.stack([lax.axis_index(Y), lax.axis_index(Z), back]).astype(jnp.int32)
    out, row_high, row_low = near_product(where, rows, *units[:6])
    return far_product(where, row_high, row_low, *units[6:], out)


def solution(mesh):
    fine = Mesh(mesh.devices.reshape(SIZES), ALL)
    in_spec = P(DAY, None, GROUP)
    return jax.shard_map(
        body,
        mesh=fine,
        in_specs=(in_spec, in_spec),
        out_specs=P(DAY, (Y, Z), (X, CORE)),
        check_vma=False,
    )
```

```python
import jax
import jax.numpy as jnp
from jax import lax
from jax.experimental import pallas as pl
from jax.experimental.pallas import tpu as pltpu
from jax.sharding import Mesh
from jax.sharding import PartitionSpec as P

DAY, Y, Z, X, CORE = "day", "y", "z", "x", "core"
SIZES = (4, 4, 4, 4, 2)
ALL = (DAY, Y, Z, X, CORE)
GROUP = (Y, Z, X, CORE)
N = 4
WHOLE = pl.BlockSpec(memory_space=pltpu.VMEM)
SCALARS = pl.BlockSpec(memory_space=pltpu.SMEM)


def turn_pairs():
    def place(y, z, x, core):
        return ((y * N + z) * N + x) * 2 + core

    pairs = []
    for y in range(N):
        for z in range(N):
            for x in range(N):
                for core in range(2):
                    pairs.append((place(y, z, x, core), place(x, (z % 2) * 2 + core, y, z // 2)))
    return pairs


def shift(step):
    return [(i, (i + step) % N) for i in range(N)]


def ring_pairs():
    return [(y * 2 + core, (y + (1, N - 1)[core]) % N * 2 + core) for y in range(N) for core in range(2)]


def local(kernel, shapes, *blocks, after=(), specs=None, scratch=()):
    skip = len(after)

    def run(*refs):
        kernel(*refs[: len(blocks)], *refs[len(blocks) + skip :])

    moved = sum(4 * block.size for block in blocks) + sum(4 * shape.size for shape in shapes)
    return pl.pallas_call(
        run,
        in_specs=(specs or [WHOLE] * len(blocks)) + [pl.BlockSpec(memory_space=pl.ANY)] * skip,
        out_specs=[WHOLE] * len(shapes),
        out_shape=shapes,
        scratch_shapes=scratch,
        compiler_params=pltpu.CompilerParams(vmem_limit_bytes=8 * 1024 * 1024),
        cost_estimate=pl.CostEstimate(flops=moved, bytes_accessed=moved, transcendentals=0),
    )(*blocks, *after)


def sums_kernel(returns_far, traded_far, masked, sums, returns, traded, sems):
    copies = [
        pltpu.make_async_copy(returns_far, returns, sems.at[0]),
        pltpu.make_async_copy(traded_far, traded, sems.at[1]),
    ]
    for copy in copies:
        copy.start()
    for copy in copies:
        copy.wait()
    share = sums.shape[2]
    for group in range(N):
        rows = slice(group * share, (group + 1) * share)
        absolute = jnp.zeros(sums.shape[2:], jnp.float32)
        count = jnp.zeros(sums.shape[2:], jnp.float32)
        for k in range(masked.shape[0]):
            live = traded[k, rows, :].astype(jnp.float32)
            value = live * returns[k, rows, :]
            masked[k, rows, :] = value
            absolute += jnp.abs(value)
            count += live
        sums[group, 0] = absolute
        sums[group, 1] = count


def weight_kernel(sums, weight):
    absolute = (sums[0, 0] + sums[1, 0]) + (sums[2, 0] + sums[3, 0])
    count = (sums[0, 1] + sums[1, 1]) + (sums[2, 1] + sums[3, 1])
    level = absolute / jnp.maximum(count, 1.0)
    profile = level / jnp.sqrt(jnp.mean(level * level, axis=1, keepdims=True) + 1e-06)
    weight[...] = 1.0 / jnp.maximum(profile, 0.2)


def scale_kernel(masked, weight, scaled):
    for k in range(masked.shape[0]):
        scaled[k] = masked[k] * weight[...]


def pair_kernel(first, second, out):
    out[:2] = first[...]
    out[2:] = second[...]


def split(value):
    high = value.astype(jnp.bfloat16)
    low = (value - high.astype(jnp.float32)).astype(jnp.bfloat16)
    return high, low


def triple(row_high, row_low, col_high, col_low):
    def dot(left, right):
        return lax.dot_general(left, right, (((1,), (1,)), ((), ())), preferred_element_type=jnp.float32)

    return dot(row_high, col_low) + dot(row_low, col_high) + dot(row_high, col_high)


def keep_columns(where, step, blocks, high, low):
    size = blocks[0].shape[0]
    for n, block in enumerate(blocks):
        part = pl.ds(pl.multiple_of(lax.rem(where[1] - n + N, N) * size, size), size)
        high[step, part, :], low[step, part, :] = split(block)


def send_columns(where, step, k, tile, out, sems):
    half = tile.shape[1] // 2
    x = lax.rem(where[0] + step * where[2], N)
    copies = []
    for p in range(2):
        start = pl.multiple_of((p * N + x) * half, half)
        copies.append(
            pltpu.make_async_copy(tile.at[:, p * half : (p + 1) * half], out.at[k, :, pl.ds(start, half)], sems.at[p])
        )
    return copies


def near_kernel(
    where, rows, a, b, a_one, b_one, a_two, b_two, out, row_high, row_low, high, low, tiles, sems
):
    size = rows.shape[2]
    copies = []
    for k in range(2):
        for n in range(rows.shape[0]):
            part = slice(n * size, (n + 1) * size)
            row_high[k, part, :], row_low[k, part, :] = split(rows[n, k])
        for step, (here, there) in enumerate(((a, b), (a_one, b_one), (a_two, b_two))):
            blocks = [there[k], there[2 + k], here[k], here[2 + k]]
            spot = 3 * k + step
            keep_columns(where, spot, blocks, high, low)
            tiles[k, step] = triple(row_high[k], row_low[k], high[spot], low[spot])
            for copy in send_columns(where, step, k, tiles.at[k, step], out, sems.at[k, step]):
                copy.start()
                copies.append(copy)
    for copy in copies:
        copy.wait()


def far_kernel(where, row_high, row_low, a, b, kept, out, high, low, tiles, sems):
    copies = []
    for k in range(2):
        keep_columns(where, k, [b[k], b[2 + k], a[k], a[2 + k]], high, low)
        tiles[k] = triple(row_high[k], row_low[k], high[k], low[k])
        for copy in send_columns(where, 3, k, tiles.at[k], out, sems.at[k]):
            copy.start()
            copies.append(copy)
    for copy in copies:
        copy.wait()


def near_product(where, rows, *blocks):
    _, days, size, bins = rows.shape
    height, width = rows.shape[0] * size, N * size
    halves = [jax.ShapeDtypeStruct((days, height, bins), jnp.bfloat16)] * 2
    return pl.pallas_call(
        near_kernel,
        in_specs=[SCALARS] + [WHOLE] * (1 + len(blocks)),
        out_specs=[pl.BlockSpec(memory_space=pl.ANY), WHOLE, WHOLE],
        out_shape=[jax.ShapeDtypeStruct((days, height, N * width), jnp.float32)] + halves,
        scratch_shapes=[
            pltpu.VMEM((3 * days, width, bins), jnp.bfloat16),
            pltpu.VMEM((3 * days, width, bins), jnp.bfloat16),
            pltpu.VMEM((days, 3, height, width), jnp.float32),
            pltpu.SemaphoreType.DMA((days, 3, 2)),
        ],
        compiler_params=pltpu.CompilerParams(vmem_limit_bytes=16 * 1024 * 1024),
        cost_estimate=pl.CostEstimate(
            flops=18 * days * height * width * bins, bytes_accessed=12 * days * height * width, transcendentals=0
        ),
    )(where, rows, *blocks)


def far_product(where, row_high, row_low, a, b, kept):
    days, height, bins = row_high.shape
    width = kept.shape[2] // N
    anywhere = pl.BlockSpec(memory_space=pl.ANY)
    return pl.pallas_call(
        far_kernel,
        in_specs=[SCALARS] + [WHOLE] * 4 + [anywhere],
        out_specs=anywhere,
        out_shape=jax.ShapeDtypeStruct(kept.shape, kept.dtype),
        input_output_aliases={5: 0},
        scratch_shapes=[
            pltpu.VMEM((days, width, bins), jnp.bfloat16),
            pltpu.VMEM((days, width, bins), jnp.bfloat16),
            pltpu.VMEM((days, height, width), jnp.float32),
            pltpu.SemaphoreType.DMA((days, 2)),
        ],
        compiler_params=pltpu.CompilerParams(vmem_limit_bytes=8 * 1024 * 1024),
        cost_estimate=pl.CostEstimate(
            flops=6 * days * height * width * bins, bytes_accessed=4 * days * height * width, transcendentals=0
        ),
    )(where, row_high, row_low, a, b, kept)


def body(returns, traded):
    returns = jnp.swapaxes(returns, 1, 2)
    traded = jnp.swapaxes(traded, 1, 2)
    days, size, bins = returns.shape
    share = size // N

    def shape(*sizes):
        return jax.ShapeDtypeStruct(sizes, jnp.float32)

    masked, sums = local(
        sums_kernel,
        [shape(days, size, bins), shape(N, 2, share, bins)],
        returns,
        traded,
        specs=[pl.BlockSpec(memory_space=pltpu.HBM)] * 2,
        scratch=[
            pltpu.VMEM((days, size, bins), jnp.float32),
            pltpu.VMEM((days, size, bins), jnp.int32),
            pltpu.SemaphoreType.DMA((2,)),
        ],
    )
    sums = lax.all_to_all(sums, DAY, 0, 0)
    (weight,) = local(weight_kernel, [shape(share, bins)], sums)
    weight = lax.all_gather(weight, DAY, axis=0, tiled=True)
    (scaled,) = local(scale_kernel, [shape(days, size, bins)], masked, weight)

    rows = lax.all_gather(scaled, (X, CORE))

    turned = lax.ppermute(scaled, GROUP, turn_pairs())
    z1, z3 = [lax.ppermute(turned, Z, shift(step)) for step in (1, 3)]
    z2 = lax.ppermute(z1, Z, shift(1))
    (b,) = local(pair_kernel, [shape(4, size, bins)], turned, z1)
    (a,) = local(pair_kernel, [shape(4, size, bins)], z2, z3)
    units = [a, b]
    for _ in range(N - 1):
        units += [lax.ppermute(unit, (Y, CORE), ring_pairs()) for unit in units[-2:]]

    back = lax.select(lax.axis_index(CORE) == 0, N - 1, 1)
    where = jnp.stack([lax.axis_index(Y), lax.axis_index(Z), back]).astype(jnp.int32)
    out, row_high, row_low = near_product(where, rows, *units[:6])
    return far_product(where, row_high, row_low, *units[6:], out)


def solution(mesh):
    fine = Mesh(mesh.devices.reshape(SIZES), ALL)
    in_spec = P(DAY, None, GROUP)
    return jax.shard_map(
        body,
        mesh=fine,
        in_specs=(in_spec, in_spec),
        out_specs=P(DAY, (Y, Z), (X, CORE)),
        check_vma=False,
    )
```
